128 devices in a mesh: dp: 32 (over z, y, core), ctx: 4 (over x).
Axes of the slice: x: 4, y: 4, z: 4, core: 2. Of those that a mesh axis runs over, the one named last changes fastest.
Arguments:
- queries: bfloat16 [90112, 2048], P(('dp', 'ctx')), may hold values from -8 to 8
- keys: bfloat16 [90112, 512], P(('dp', 'ctx')), may hold values from -8 to 8
- values: bfloat16 [90112, 512], P(('dp', 'ctx')), may hold values from -6 to 6
- out_grad: bfloat16 [90112, 2048], P(('dp', 'ctx')), may hold values from -6 to 6
- short_lengths: int32 [128, 4], P(('dp', 'ctx')), may hold values from 1 to 64, 128 in all within a row
- doc_lengths: int32 [64], replicated, may hold values from 0 to 2304, as said below
- doc_group: int32 [64], replicated, may hold values from 0 to 31
- doc_offset: int32 [64], replicated, may hold values from 0 to 2304, as said below
Outputs:
- attended: bfloat16 [90112, 2048], P(('dp', 'ctx'))
- query_grads: bfloat16 [90112, 2048], P(('dp', 'ctx'))
- key_grads: bfloat16 [90112, 512], P(('dp', 'ctx'))
- value_grads: bfloat16 [90112, 512], P(('dp', 'ctx'))
The draws below stay inside these ranges and needn't reach their ends.
Inputs may be any that keep to these rules, and one draw needn't show every extreme that they name: `short_lengths`: each row sums to 128. `doc_lengths`: each group is named by exactly 2 documents; the nonempty documents of a group tile its positions 0 to 4 * 576 - 1 without gaps; every length is 0 or a multiple of 4 * 32 and at least 8 times that. `doc_offset`: an empty document has offset 4 * 576.
All inputs are finite; a program needn't handle non-finite values.
Results may differ from the reference program's by a relative error of at most 0.0054.
The reference program's roundings to bfloat16 on the way (of `weights` and `score_grads`) count: a program that leaves them out, or rounds other values in their place, can miss the bound.
Values may be sent and summed in bfloat16 or wider, within the bound.
A program may use at most 192 MiB of HBM per device.

```python
import math
import jax
import jax.numpy as jnp
import numpy as np
from jax import lax

HQ = 16
HK = 4
DH = 128
SHORT_DEV = 128
LONG_DEV = 576
SHORT_DOCS = 4
TOKENS = 90112
N_DP = 32
N_CTX = 4


def draw_queries(key, part):
    key = jax.random.fold_in(key, 1)
    drawn = jnp.clip(jax.random.normal(key, (TOKENS, HQ * DH), jnp.float32), -6.0, 6.0)
    return drawn.astype(jnp.bfloat16)


def draw_keys(key, part):
    key = jax.random.fold_in(key, 2)
    drawn = jnp.clip(jax.random.normal(key, (TOKENS, HK * DH), jnp.float32), -6.0, 6.0)
    return drawn.astype(jnp.bfloat16)


def long_documents(key):
    key = jax.random.fold_in(key, 202)
    kind_key, cut_key, force_key, order_key = jax.random.split(key, 4)
    kinds = jax.random.randint(kind_key, (N_DP,), 0, 2)
    forced = jax.random.randint(force_key, (), 0, N_DP)
    kinds = jnp.where(jnp.arange(N_DP) == forced, 0, kinds)
    cuts = jax.random.randint(cut_key, (N_DP,), 8, 11)
    unit = N_CTX * LONG_DEV // 18
    first = jnp.where(kinds == 0, 18, cuts)
    second = jnp.where(kinds == 0, 0, 18 - cuts)
    slot_lengths = jnp.stack([first, second], axis=1) * unit
    slot_offsets = jnp.stack([jnp.zeros_like(first), first], axis=1) * unit
    slot_offsets = jnp.where(slot_lengths == 0, 18 * unit, slot_offsets)
    slot_groups = jnp.broadcast_to(jnp.arange(N_DP)[:, None], (N_DP, 2))
    order = jax.random.permutation(order_key, N_DP * 2)
    return (slot_lengths.reshape(-1)[order].astype(jnp.int32), slot_groups.reshape(-1)[order].astype(jnp.int32), slot_offsets.reshape(-1)[order].astype(jnp.int32))


def draw_doc_lengths(key, part):
    return long_documents(key)[0]


def draw_doc_group(key, part):
    return long_documents(key)[1]


def draw_doc_offset(key, part):
    return long_documents(key)[2]


def block_levels(stream_key, dims, cuts, least, high):
    factor_of = 1.0
    for dim, parts in cuts:
        heights = jax.random.uniform(jax.random.fold_in(jax.random.fold_in(stream_key, 6), dim), (parts,), jnp.float32, least / len(cuts), high / len(cuts))
        factor_of = factor_of * jnp.repeat(jnp.exp(heights), dims[dim] // parts).reshape((-1,) + (1,) * (len(dims) - 1 - dim))
    return factor_of


def split_up(number_of, total, most, slope):
    weights = [(1 << 20) // math.isqrt(standing ** slope) + 1 for standing in range(2, number_of + 1)]
    rest, holding = total - most - (number_of - 1), [1] * (number_of - 1)
    while rest > 0:
        free = [i for i in range(number_of - 1) if holding[i] < most]
        mass, budget = sum([weights[i] for i in free]), rest
        for i in free:
            extra = min(most - holding[i], max(1, budget * weights[i] // mass), rest)
            holding[i] = holding[i] + extra
            rest = rest - extra
    return np.array([most] + holding)


def uneven(key, amount, total, bound, slope):
    if amount == 2:
        one = jax.random.randint(key, (), max(1, total - bound), min(bound, total - 1) + 1)
        return jnp.stack([one, total - one])
    tallies = jnp.asarray(split_up(amount, total, bound, slope), jnp.int32)
    couples = (amount - 1) // 2
    donor, sink = tallies[1:1 + 2 * couples:2], tallies[2:2 + 2 * couples:2]
    margin = jnp.minimum(donor - 1, bound - sink)
    passed = jax.random.randint(jax.random.fold_in(key, 1), (couples,), 0, 1 << 20) % (margin + 1)
    tallies = tallies.at[1:1 + 2 * couples:2].set(donor - passed).at[2:2 + 2 * couples:2].set(sink + passed)
    return tallies[jax.random.permutation(jax.random.fold_in(key, 2), amount)]


def gaussian(rng, dims, spread, reach, cuts=(), kind=jnp.bfloat16):
    level = block_levels(rng, dims, cuts, -0.22, 0.18) if cuts else 1.0
    values = jax.random.normal(rng, dims, jnp.float32) * spread * level
    return jnp.minimum(jnp.maximum(values, -reach), reach).astype(kind)


def setup_inputs(seed: int = 0) -> dict:
    arg_keys = jax.random.split(jax.random.key(seed), 9)
    queries = draw_queries(jax.random.fold_in(arg_keys[8], 71), 0)
    keys = draw_keys(jax.random.fold_in(arg_keys[8], 71), 0)
    values = gaussian(arg_keys[2], (TOKENS, HK * DH), 1.0, 6.0, ((0, 128),))
    out_grad = gaussian(arg_keys[3], (TOKENS, HQ * DH), 1.0, 6.0, ((0, 128),))
    short_lengths = jax.vmap(lambda own: uneven(own, SHORT_DOCS, SHORT_DEV, SHORT_DEV // 2, 2))(jax.random.split(arg_keys[4], (N_DP * N_CTX))).reshape((N_DP * N_CTX, SHORT_DOCS)).astype(jnp.int32)
    doc_lengths = draw_doc_lengths(jax.random.fold_in(arg_keys[8], 71), 0)
    doc_group = draw_doc_group(jax.random.fold_in(arg_keys[8], 71), 0)
    doc_offset = draw_doc_offset(jax.random.fold_in(arg_keys[8], 71), 0)
    return {"queries": queries, "keys": keys, "values": values, "out_grad": out_grad, "short_lengths": short_lengths, "doc_lengths": doc_lengths, "doc_group": doc_group, "doc_offset": doc_offset}


MASKED = -1e+30

def rounded(numbers):
    return lax.optimization_barrier(numbers.astype(jnp.bfloat16)).astype(jnp.float32)

def short_segments(lengths, count):
    ends = jnp.cumsum(lengths, dtype=jnp.int32)
    positions = jnp.arange(count, dtype=jnp.int32)
    return lax.optimization_barrier(jnp.sum((positions[:, None] >= ends[None, :]).astype(jnp.int32), axis=1, dtype=jnp.int32))

def doc_segments(positions, group_id, doc_lengths, doc_group, doc_offset):
    inside = (doc_group[None, :] == group_id) & (positions[:, None] >= doc_offset[None, :]) & (positions[:, None] < doc_offset[None, :] + doc_lengths[None, :])
    labels = jnp.arange(1, doc_lengths.shape[0] + 1, dtype=jnp.int32)
    return lax.optimization_barrier(jnp.sum(jnp.where(inside, labels[None, :], 0), axis=1, dtype=jnp.int32))

def head_grads(head_query, head_key, head_value, head_grad, allowed):
    scaling = 1.0 / math.sqrt(DH)
    scores = jnp.einsum('rgd,sd->grs', head_query, head_key) * scaling
    scores = jnp.where(allowed[None], scores, MASKED)
    row_max = lax.optimization_barrier(jnp.max(scores, axis=2, keepdims=True))
    log_total = row_max + jnp.log(lax.optimization_barrier(jnp.sum(jnp.exp(scores - row_max), axis=2, keepdims=True)))
    weights_full = jnp.exp(scores - log_total)
    weights = rounded(weights_full)
    head_out = rounded(jnp.einsum('grs,sd->rgd', weights, head_value))
    products = lax.optimization_barrier(jnp.sum(head_grad * head_out, axis=2)).T
    value_part = jnp.einsum('grs,rgd->sd', weights, head_grad)
    weight_grads = jnp.einsum('rgd,sd->grs', head_grad, head_value)
    score_grads = rounded(weights_full * (weight_grads - products[:, :, None]))
    query_part = jnp.einsum('grs,sd->rgd', score_grads, head_key) * scaling
    key_part = jnp.einsum('grs,rgd->sd', score_grads, head_query) * scaling
    return (head_out, query_part, key_part, value_part)

def attend(query_rows, key_rows, value_rows, grad_rows, allowed):
    row_count = query_rows.shape[0]
    key_count = key_rows.shape[0]
    per_group = HQ // HK
    query_heads = query_rows.astype(jnp.float32).reshape(row_count, HK, per_group, DH).transpose(1, 0, 2, 3)
    grad_heads = grad_rows.astype(jnp.float32).reshape(row_count, HK, per_group, DH).transpose(1, 0, 2, 3)
    key_heads = key_rows.astype(jnp.float32).reshape(key_count, HK, DH).transpose(1, 0, 2)
    value_heads = value_rows.astype(jnp.float32).reshape(key_count, HK, DH).transpose(1, 0, 2)

    def one_head(operands):
        return head_grads(operands[0], operands[1], operands[2], operands[3], allowed)
    outputs, query_part, key_part, value_part = lax.map(one_head, (query_heads, key_heads, value_heads, grad_heads))
    outputs = outputs.transpose(1, 0, 2, 3).reshape(row_count, HQ * DH)
    query_part = query_part.transpose(1, 0, 2, 3).reshape(row_count, HQ * DH)
    key_part = key_part.transpose(1, 0, 2).reshape(key_count, HK * DH)
    value_part = value_part.transpose(1, 0, 2).reshape(key_count, HK * DH)
    return (outputs, query_part, key_part, value_part)

def reference(queries, keys, values, out_grad, short_lengths, doc_lengths, doc_group, doc_offset):
    shards = N_DP * N_CTX
    row_count = SHORT_DEV + LONG_DEV
    piece = LONG_DEV // N_DP
    group_span = N_CTX * LONG_DEV
    half = LONG_DEV // 2

    def split(array):
        array = array.reshape(shards, row_count, array.shape[1])
        return (array[:, :SHORT_DEV], array[:, SHORT_DEV:])

    def to_groups(array):
        width = array.shape[2]
        return array.reshape(N_DP, N_CTX, N_DP, piece, width).transpose(2, 1, 0, 3, 4).reshape(N_DP, group_span, width)

    def to_shards(array):
        width = array.shape[2]
        return array.reshape(N_DP, N_CTX, N_DP, piece, width).transpose(2, 1, 0, 3, 4).reshape(shards, LONG_DEV, width)
    local_index = jnp.arange(group_span, dtype=jnp.int32)
    member_of = local_index // LONG_DEV
    member_row = local_index % LONG_DEV
    group_positions = jnp.where(member_row < half, member_of * half + member_row, (2 * N_CTX - 1 - member_of) * half + member_row - half).astype(jnp.int32)
    short_query, long_query = split(queries)
    short_key, long_key = split(keys)
    short_value, long_value = split(values)
    short_grad, long_grad = split(out_grad)

    def short_one(operands):
        lengths, query_rows, key_rows, value_rows, grad_rows = operands
        segments = short_segments(lengths, SHORT_DEV)
        positions = jnp.arange(SHORT_DEV, dtype=jnp.int32)
        allowed = (segments[:, None] == segments[None, :]) & (positions[None, :] <= positions[:, None])
        return attend(query_rows, key_rows, value_rows, grad_rows, allowed)
    short_results = lax.map(short_one, (short_lengths, short_query, short_key, short_value, short_grad))

    def long_one(operands):
        group_id, query_rows, key_rows, value_rows, grad_rows = operands
        segments = doc_segments(group_positions, group_id, doc_lengths, doc_group, doc_offset)
        allowed = (segments[:, None] == segments[None, :]) & (group_positions[None, :] <= group_positions[:, None])
        return attend(query_rows, key_rows, value_rows, grad_rows, allowed)
    long_results = lax.map(long_one, (jnp.arange(N_DP, dtype=jnp.int32), to_groups(long_query), to_groups(long_key), to_groups(long_value), to_groups(long_grad)))

    def assemble(short_part, long_part):
        whole = jnp.concatenate([short_part, to_shards(long_part)], axis=1)
        return whole.reshape(shards * row_count, whole.shape[2]).astype(jnp.bfloat16)
    return (assemble(short_results[0], long_results[0]), assemble(short_results[1], long_results[1]), assemble(short_results[2], long_results[2]), assemble(short_results[3], long_results[3]))
```

```python
import functools
import math

import jax
import jax.numpy as jnp
from jax import lax
from jax.experimental import pallas as pl
from jax.experimental.pallas import tpu as pltpu
from jax.sharding import PartitionSpec as P

HQ = 16
HK = 4
DH = 128
SHORT_DEV = 128
LONG_DEV = 576
ROWS = SHORT_DEV + LONG_DEV

N_DEV = 128
GROUPS = 32
PIECE = LONG_DEV // GROUPS
SLAB = 8 * PIECE
SPAN = N_DEV * PIECE
PAIR = 2
TILE = 768
SUB = 256
ROWS_A = 112
ROWS_B = 72

SCALE = 1.0 / math.sqrt(DH)
SCALE2 = math.log2(math.e) / math.sqrt(DH)
MASKED = -1e30
FAR = 1 << 20
F32 = jnp.float32
BF16 = jnp.bfloat16
MESH = pl.DeviceIdType.MESH


def dot(a, b, dim_a, dim_b):
    return lax.dot_general(
        a, b, (((dim_a,), (dim_b,)), ((), ())), preferred_element_type=F32
    )


def by_eight(x):
    return x.reshape(x.shape[0] // 8, 8, x.shape[1])


def over_rows(x, op):
    return jnp.broadcast_to(op(x, axis=0, keepdims=True), (8, x.shape[1]))


def position_of(dp, ctx):
    return jnp.where(dp < 16, ctx * 16 + dp, (7 - ctx) * 16 + dp - 16)


TURNS = ((1, 0), (0, 1), (3, 0), (0, 3), (1, 3), (3, 1), (2, 2), (0, 2),
         (2, 0), (1, 1), (3, 3), (1, 2), (3, 2), (2, 1), (2, 3), (0, 0))


def each_partner(dp, ctx, body):
    def wrap(value, size):
        return jnp.where(value >= size, value - size, value)

    xs = [wrap(ctx + i, 4) for i in range(4)]
    ys = [wrap(lax.rem(dp // 2, 4) + i, 4) * 2 for i in range(4)]

    def turn(j, turns):
        z = wrap(dp // 8 + lax.rem(j, 4), 4)
        core = wrap(lax.rem(dp, 2) + j // 4, 2)
        zs = [wrap(z + i, 4) * 8 for i in range(4)]
        cores = [core, 1 - core]
        for x, y in turns:
            body(zs[(x + y) % 4] + ys[y] + cores[x % 2], xs[x])

    def step(j, carry):
        turn(j, TURNS)
        return carry

    turn(0, TURNS[:-1])
    lax.fori_loop(1, 8, step, 0)


def attend_tile(i, bound, q_ref, g_ref, k_ref, v_ref, kt_ref, vt_ref, o_ref, dq_ref,
                dk_acc, dv_acc, s_buf, o_acc, dq_acc):
    subs = TILE // SUB
    wide = PAIR * SUB
    total = PAIR * TILE
    start = pl.multiple_of(i * TILE, TILE)

    def at(a):
        return pl.ds(pl.multiple_of(start + a * SUB, SUB), SUB)

    def gather(ref):
        return jnp.concatenate([ref[h, at(a), :] for a in range(subs) for h in range(PAIR)], 0)

    q = gather(q_ref)
    g = gather(g_ref)
    row = start + jnp.concatenate(
        [lax.broadcasted_iota(jnp.int32, (8, SUB), 1) + a * SUB
         for a in range(subs) for _ in range(PAIR)], 1)

    def scores(k0, count, first, diagonal, maxima):
        lane0 = first * wide
        maxima = list(maxima)
        for t in range(0, count, 128):
            c0 = pl.multiple_of(k0 + t, 128)
            s = by_eight(dot(k_ref[pl.ds(c0, 128), :], q[lane0:], 1, 1))
            limit = jnp.where(c0 < bound, bound, FAR)
            s = s + jnp.where(row[:, lane0:] >= limit, MASKED, 0.0)[None]
            for a in range(first, subs):
                part = s[:, :, (a - first) * wide:(a - first + 1) * wide]
                if diagonal and a == first:
                    key = (lax.broadcasted_iota(jnp.int32, part.shape, 0) * 8
                           + lax.broadcasted_iota(jnp.int32, part.shape, 1) + c0)
                    part = jnp.where(key > row[None, :, a * wide:(a + 1) * wide], MASKED, part)
                s_buf[pl.ds(c0, 128), a * wide:(a + 1) * wide] = part.reshape(128, wide)
                maxima[a] = jnp.maximum(maxima[a], jnp.max(part, axis=0))
        return tuple(maxima)

    def sweep(body, carry):
        carry = lax.fori_loop(
            0, i, lambda kb, x: body(pl.multiple_of(kb * TILE, TILE), TILE, 0, False, x), carry)
        for a in range(subs):
            carry = body(pl.multiple_of(start + a * SUB, SUB), SUB, a, True, carry)
        return carry

    maxima = sweep(scores, tuple(jnp.full((8, wide), MASKED, F32) for _ in range(subs)))
    top = jnp.concatenate([over_rows(x, jnp.max) * SCALE2 for x in maxima], 1)

    def powers(k0, count, first, diagonal, sums):
        lane0 = first * wide
        p = jnp.exp2(by_eight(s_buf[pl.ds(k0, count), lane0:]) * SCALE2 - top[None, :, lane0:])
        s_buf[pl.ds(k0, count), lane0:] = p.reshape(count, total - lane0)
        added = jnp.sum(p, axis=0)
        return tuple(
            x if a < first else x + added[:, (a - first) * wide:(a - first + 1) * wide]
            for a, x in enumerate(sums))

    sums = sweep(powers, tuple(jnp.zeros((8, wide), F32) for _ in range(subs)))
    inverse = jnp.concatenate([1.0 / over_rows(x, jnp.sum) for x in sums], 1)

    o_acc[...] = jnp.zeros_like(o_acc)

    def outputs(k0, count, first, diagonal, carry):
        lane0 = first * wide
        w = by_eight(s_buf[pl.ds(k0, count), lane0:]) * inverse[None, :, lane0:]
        w = w.reshape(count, total - lane0).astype(BF16)
        o_acc[:, lane0:] += dot(vt_ref[:, pl.ds(k0, count)], w, 1, 0)
        dv_acc[pl.ds(k0, count), :] += dot(w, g[lane0:], 1, 0)
        return carry

    sweep(outputs, 0)
    out = o_acc[...].astype(BF16)

    def put(ref, x):
        x = x.T
        for a in range(subs):
            for h in range(PAIR):
                ref[h, at(a), :] = x[(a * PAIR + h) * SUB:(a * PAIR + h + 1) * SUB]

    put(o_ref, out)
    product = over_rows(g.T.astype(F32) * out.astype(F32), jnp.sum)
    dq_acc[...] = jnp.zeros_like(dq_acc)

    def backward(k0, count, first, diagonal, carry):
        lane0 = first * wide
        dp = by_eight(dot(v_ref[pl.ds(k0, count), :], g[lane0:], 1, 1))
        w = by_eight(s_buf[pl.ds(k0, count), lane0:]) * inverse[None, :, lane0:]
        ds = (w * (dp - product[None, :, lane0:])).reshape(count, total - lane0).astype(BF16)
        dq_acc[:, lane0:] += dot(kt_ref[:, pl.ds(k0, count)], ds, 1, 0)
        dk_acc[pl.ds(k0, count), :] += dot(ds, q[lane0:], 1, 0)
        return carry

    sweep(backward, 0)
    put(dq_ref, (dq_acc[...] * SCALE).astype(BF16))


def attend_short(lengths_ref, q_ref, k_ref, v_ref, g_ref, o_ref, dq_ref, dk_ref, dv_ref):
    heads = HQ // HK
    lanes = heads * SHORT_DEV
    key = lax.broadcasted_iota(jnp.int32, (SHORT_DEV, lanes), 0)
    row = jnp.concatenate(
        [lax.broadcasted_iota(jnp.int32, (SHORT_DEV, SHORT_DEV), 1)] * heads, 1)
    end = 0
    key_segment = jnp.zeros_like(key)
    row_segment = jnp.zeros_like(row)
    for j in range(4):
        end = end + lengths_ref[0, j]
        key_segment = key_segment + (key >= end).astype(jnp.int32)
        row_segment = row_segment + (row >= end).astype(jnp.int32)
    masked = jnp.where((key > row) | (key_segment != row_segment), MASKED, 0.0)

    def one(c, carry):
        mine = pl.ds(pl.multiple_of(c * DH, DH), DH)

        def col(h):
            return pl.ds(pl.multiple_of((c * heads + h) * DH, DH), DH)

        def gather(ref):
            return jnp.concatenate([ref[:SHORT_DEV, col(h)] for h in range(heads)], 0)

        q = gather(q_ref)
        g = gather(g_ref)
        k = k_ref[:SHORT_DEV, mine]
        v = v_ref[:SHORT_DEV, mine]
        s = dot(k, q, 1, 1) + masked
        p = jnp.exp2((s - jnp.max(s, axis=0, keepdims=True)) * SCALE2)
        weights = p * (1.0 / jnp.sum(p, axis=0, keepdims=True))
        w = weights.astype(BF16)
        out = dot(v.T, w, 1, 0).astype(BF16)
        dv_ref[:, mine] = dot(w, g, 1, 0).astype(BF16)
        product = jnp.sum(g.T.astype(F32) * out.astype(F32), axis=0, keepdims=True)
        ds = (weights * (dot(v, g, 1, 1) - product)).astype(BF16)
        dq = (dot(k.T, ds, 1, 0) * SCALE).astype(BF16)
        dk_ref[:, mine] = (dot(ds, q, 1, 0) * SCALE).astype(BF16)
        out = out.T
        dq = dq.T
        for h in range(heads):
            o_ref[:, col(h)] = out[h * SHORT_DEV:(h + 1) * SHORT_DEV]
            dq_ref[:, col(h)] = dq[h * SHORT_DEV:(h + 1) * SHORT_DEV]
        return carry

    lax.fori_loop(0, HK, one, 0)


def kernel(lengths_ref, doc_len_ref, doc_group_ref, doc_off_ref, q_hbm, k_hbm, v_hbm, g_hbm,
           back_a, back_b, so_ref, sdq_ref, sdk_ref, sdv_ref,
           q_ref, k_ref, v_ref, g_ref, send_a, send_b, got_a, got_b, qd, gd, kd, vd, kt, vt, od, dqd,
           dk_acc, dv_acc, s_buf, o_acc, dq_acc, edge,
           send_sem, recv_sem, own_sem, load_sem):
    dp = lax.axis_index("dp")
    ctx = lax.axis_index("ctx")
    me = dp * 4 + ctx
    my_place = position_of(dp, ctx)
    barrier = pltpu.get_barrier_semaphore()

    def greet(*to):
        pl.semaphore_signal(barrier, inc=1, device_id=to, device_id_type=MESH)

    each_partner(dp, ctx, greet)
    loads = [
        pltpu.make_async_copy(src, dst, load_sem.at[n])
        for n, (src, dst) in enumerate(
            ((q_hbm, q_ref), (g_hbm, g_ref), (k_hbm, k_ref), (v_hbm, v_ref)))]
    for load in loads:
        load.start()

    def pack(out, first, with_keys):
        def body(b, carry):
            base = pl.multiple_of(SHORT_DEV + SLAB * b, 16)
            for c in range(HK):
                col = (c * (HQ // HK) + first) * DH
                parts = [(q_ref, col), (q_ref, col + DH), (g_ref, col), (g_ref, col + DH)]
                if with_keys:
                    parts += [(k_ref, c * DH), (v_ref, c * DH)]
                for n, (ref, at) in enumerate(parts):
                    x = ref[pl.ds(base, SLAB), at:at + DH]
                    for j in range(8):
                        out[(b * 8 + j) * 4 + c, PIECE * n:PIECE * (n + 1), :] = (
                            x[PIECE * j:PIECE * (j + 1)])
            return carry

        lax.fori_loop(0, GROUPS // 8, body, 0)

    def exchange(slot, src, dst, src_index, dst_index):
        def send(*to):
            pltpu.make_async_remote_copy(
                src_ref=src.at[src_index(*to)], dst_ref=dst.at[dst_index],
                send_sem=send_sem.at[slot], recv_sem=recv_sem.at[slot],
                device_id=to, device_id_type=MESH).start()

        each_partner(dp, ctx, send)
        pltpu.make_async_copy(
            src.at[src_index(dp, ctx)], dst.at[dst_index], own_sem.at[slot]).start()

    def wait_bytes(ref, sem):
        whole = ref.at[pl.ds(0, N_DEV - 1)]
        pltpu.make_async_copy(whole, whole, sem).wait()

    def received(slot, src, dst):
        pltpu.make_async_copy(src.at[0], dst.at[0], own_sem.at[slot]).wait()
        wait_bytes(dst, recv_sem.at[slot])

    send_a[:, 96:, :] = jnp.zeros((N_DEV, ROWS_A - 96, DH), BF16)
    for load in loads:
        load.wait()
    pack(send_a, 0, True)
    pl.semaphore_wait(barrier, N_DEV - 1)
    exchange(0, send_a, got_a, lambda d, c: d * 4 + c, my_place)
    pack(send_b, PAIR, False)
    attend_short(lengths_ref, q_ref, k_ref, v_ref, g_ref, so_ref, sdq_ref, sdk_ref, sdv_ref)

    def find(i, acc):
        mine = (doc_group_ref[i] == dp) & (doc_len_ref[i] > 0)
        return acc + jnp.where(mine, doc_off_ref[i], 0)

    bound = lax.fori_loop(0, doc_len_ref.shape[0], find, jnp.int32(0))
    dk_acc[...] = jnp.zeros_like(dk_acc)
    dv_acc[...] = jnp.zeros_like(dv_acc)

    def spread(src, dests):
        def body(b, carry):
            at = pl.ds(pl.multiple_of(b * SLAB, 16), SLAB)
            for n, (ref, h) in enumerate(dests):
                for j in range(8):
                    edge[n, PIECE * j:PIECE * (j + 1), :] = (
                        src[b * 8 + j, PIECE * n:PIECE * (n + 1), :])
                if h is None:
                    ref[at, :] = edge[n]
                else:
                    ref[h, at, :] = edge[n]
            return carry

        lax.fori_loop(0, N_DEV // 8, body, 0)

    def collect(out, load):
        def body(b, carry):
            at = pl.ds(pl.multiple_of(b * SLAB, 16), SLAB)
            for n, x in enumerate(load(at)):
                for j in range(8):
                    out[b * 8 + j, PIECE * n:PIECE * (n + 1), :] = x[PIECE * j:PIECE * (j + 1)]
            return carry

        lax.fori_loop(0, N_DEV // 8, body, 0)

    def attend():
        def body(i, carry):
            attend_tile(i, bound, qd, gd, kd, vd, kt, vt, od, dqd,
                        dk_acc, dv_acc, s_buf, o_acc, dq_acc)
            return carry

        lax.fori_loop(0, SPAN // TILE, body, 0)

    query_side = [(qd, 0), (qd, 1), (gd, 0), (gd, 1)]
    received(0, send_a, got_a)
    exchange(1, send_b, got_b, lambda d, c: d * 4 + c, my_place)
    spread(got_a, query_side + [(kd, None), (vd, None)])
    kt[...] = kd[...].T
    vt[...] = vd[...].T
    attend()

    received(1, send_b, got_b)
    wait_bytes(send_b, send_sem.at[1])
    collect(send_b, lambda at: [od[0, at, :], od[1, at, :], dqd[0, at, :], dqd[1, at, :]])
    exchange(2, send_b, back_a, position_of, me)

    spread(got_b, query_side)
    attend()
    wait_bytes(send_a, send_sem.at[0])
    collect(send_a, lambda at: [
        od[0, at, :], od[1, at, :], dqd[0, at, :], dqd[1, at, :],
        (dk_acc[at, :] * SCALE).astype(BF16), dv_acc[at, :].astype(BF16)])
    exchange(3, send_a, back_b, position_of, me)

    received(2, send_b, back_a)
    wait_bytes(send_b, send_sem.at[2])
    received(3, send_a, back_b)
    wait_bytes(send_a, send_sem.at[3])


def place(back_a, back_b, so_ref, sdq_ref, sdk_ref, sdv_ref, o_ref, dq_ref, dk_ref, dv_ref, edge):
    o_ref[:SHORT_DEV, :] = so_ref[...]
    dq_ref[:SHORT_DEV, :] = sdq_ref[...]
    dk_ref[:SHORT_DEV, :] = sdk_ref[...]
    dv_ref[:SHORT_DEV, :] = sdv_ref[...]
    moves = []
    for half, src in enumerate((back_a, back_b)):
        for n, ref in enumerate((o_ref, o_ref, dq_ref, dq_ref)):
            moves.append((src, n, ref, (half * 2 + n % 2) * DH))
    moves += [(back_b, 4, dk_ref, 0), (back_b, 5, dv_ref, 0)]

    def body(b, carry):
        at = pl.ds(pl.multiple_of(SHORT_DEV + b * SLAB, 16), SLAB)
        for m, (src, n, ref, col) in enumerate(moves):
            for j in range(8):
                edge[m, PIECE * j:PIECE * (j + 1), :] = (
                    src[b * 8 + j, 0, PIECE * n:PIECE * (n + 1), :])
            ref[at, col:col + DH] = edge[m]
        return carry

    lax.fori_loop(0, GROUPS // 8, body, 0)


def per_device(queries, keys, values, out_grad, short_lengths, doc_lengths, doc_group, doc_offset):
    vmem = pl.BlockSpec(memory_space=pltpu.VMEM)
    smem = pl.BlockSpec(memory_space=pltpu.SMEM)
    hbm = pl.BlockSpec(memory_space=pl.ANY)

    def shape(*dims):
        return jax.ShapeDtypeStruct(dims, BF16)

    results = pl.pallas_call(
        kernel,
        out_shape=[
            shape(N_DEV, ROWS_B, DH), shape(N_DEV, ROWS_A, DH),
            shape(SHORT_DEV, HQ * DH), shape(SHORT_DEV, HQ * DH),
            shape(SHORT_DEV, HK * DH), shape(SHORT_DEV, HK * DH)],
        in_specs=[smem] * 4 + [hbm] * 4,
        out_specs=[hbm, hbm] + [vmem] * 4,
        scratch_shapes=[
            pltpu.VMEM((ROWS, HQ * DH), BF16), pltpu.VMEM((ROWS, HK * DH), BF16),
            pltpu.VMEM((ROWS, HK * DH), BF16), pltpu.VMEM((ROWS, HQ * DH), BF16),
            pltpu.VMEM((N_DEV, ROWS_A, DH), BF16), pltpu.VMEM((N_DEV, ROWS_B, DH), BF16),
            pltpu.VMEM((N_DEV, ROWS_A, DH), BF16), pltpu.VMEM((N_DEV, ROWS_B, DH), BF16),
            pltpu.VMEM((PAIR, SPAN, DH), BF16), pltpu.VMEM((PAIR, SPAN, DH), BF16),
            pltpu.VMEM((SPAN, DH), BF16), pltpu.VMEM((SPAN, DH), BF16),
            pltpu.VMEM((DH, SPAN), BF16), pltpu.VMEM((DH, SPAN), BF16),
            pltpu.VMEM((PAIR, SPAN, DH), BF16), pltpu.VMEM((PAIR, SPAN, DH), BF16),
            pltpu.VMEM((SPAN, DH), F32), pltpu.VMEM((SPAN, DH), F32),
            pltpu.VMEM((SPAN, PAIR * TILE), F32),
            pltpu.VMEM((DH, PAIR * TILE), F32), pltpu.VMEM((DH, PAIR * TILE), F32),
            pltpu.VMEM((6, SLAB, DH), BF16),
            pltpu.SemaphoreType.DMA((4,)), pltpu.SemaphoreType.DMA((4,)),
            pltpu.SemaphoreType.DMA((4,)), pltpu.SemaphoreType.DMA((4,))],
        compiler_params=pltpu.CompilerParams(
            collective_id=0, has_side_effects=True, vmem_limit_bytes=60 << 20),
        name="relay_and_attend",
    )(short_lengths, doc_lengths, doc_group, doc_offset, queries, keys, values, out_grad)

    back_a, back_b, *short = results
    heads = HQ // HK

    def back_spec(rows):
        return pl.BlockSpec((GROUPS, 1, rows, DH), lambda c: (0, c, 0, 0))

    def col_spec(rows, width):
        return pl.BlockSpec((rows, width), lambda c: (0, c))

    return tuple(pl.pallas_call(
        place,
        grid=(HK,),
        out_shape=[shape(ROWS, HQ * DH), shape(ROWS, HQ * DH),
                   shape(ROWS, HK * DH), shape(ROWS, HK * DH)],
        in_specs=[back_spec(ROWS_B), back_spec(ROWS_A),
                  col_spec(SHORT_DEV, heads * DH), col_spec(SHORT_DEV, heads * DH),
                  col_spec(SHORT_DEV, DH), col_spec(SHORT_DEV, DH)],
        out_specs=[col_spec(ROWS, heads * DH), col_spec(ROWS, heads * DH),
                   col_spec(ROWS, DH), col_spec(ROWS, DH)],
        scratch_shapes=[pltpu.VMEM((10, SLAB, DH), BF16)],
        compiler_params=pltpu.CompilerParams(vmem_limit_bytes=60 << 20),
        name="place_outputs",
    )(back_a.reshape(GROUPS, N_DEV // GROUPS, ROWS_B, DH),
      back_b.reshape(GROUPS, N_DEV // GROUPS, ROWS_A, DH), *short))


def solution(mesh):
    rows = P(("dp", "ctx"), None)
    return jax.shard_map(
        per_device, mesh=mesh,
        in_specs=(rows, rows, rows, rows, rows, P(), P(), P()),
        out_specs=(rows, rows, rows, rows), check_vma=False)
```

```python
import functools
import math

import jax
import jax.numpy as jnp
from jax import lax
from jax.experimental import pallas as pl
from jax.experimental.pallas import tpu as pltpu
from jax.sharding import PartitionSpec as P

HQ = 16
HK = 4
DH = 128
SHORT_DEV = 128
LONG_DEV = 576
ROWS = SHORT_DEV + LONG_DEV

N_DEV = 128
GROUPS = 32
PIECE = LONG_DEV // GROUPS
SLAB = 8 * PIECE
SPAN = N_DEV * PIECE
PAIR = 2
TILE = 768
SUB = 256
ROWS_A = 112
ROWS_B = 72

SCALE = 1.0 / math.sqrt(DH)
SCALE2 = math.log2(math.e) / math.sqrt(DH)
MASKED = -1e30
FAR = 1 << 20
F32 = jnp.float32
BF16 = jnp.bfloat16
MESH = pl.DeviceIdType.MESH


def dot(a, b, dim_a, dim_b):
    return lax.dot_general(
        a, b, (((dim_a,), (dim_b,)), ((), ())), preferred_element_type=F32
    )


def by_eight(x):
    return x.reshape(x.shape[0] // 8, 8, x.shape[1])


def over_rows(x, op):
    return jnp.broadcast_to(op(x, axis=0, keepdims=True), (8, x.shape[1]))


def position_of(dp, ctx):
    return jnp.where(dp < 16, ctx * 16 + dp, (7 - ctx) * 16 + dp - 16)


EARLY = 7

TURNS = ((1, 0), (0, 1), (3, 0), (0, 3), (1, 3), (3, 1), (2, 2), (0, 2),
         (2, 0), (1, 1), (3, 3), (1, 2), (3, 2), (2, 1), (2, 3), (0, 0))


def each_partner(dp, ctx, body, late=None):
    def wrap(value, size):
        return jnp.where(value >= size, value - size, value)

    xs = [wrap(ctx + i, 4) for i in range(4)]
    ys = [wrap(lax.rem(dp // 2, 4) + i, 4) * 2 for i in range(4)]

    def turn(j, turns, body):
        z = wrap(dp // 8 + lax.rem(j, 4), 4)
        core = wrap(lax.rem(dp, 2) + j // 4, 2)
        zs = [wrap(z + i, 4) * 8 for i in range(4)]
        cores = [core, 1 - core]
        for x, y in turns:
            body(zs[(x + y) % 4] + ys[y] + cores[x % 2], xs[x])

    def step(call):
        def one(j, carry):
            turn(j, TURNS, call)
            return carry

        return one

    turn(0, TURNS[:-1], body)
    lax.fori_loop(1, EARLY, step(body), 0)
    lax.fori_loop(EARLY, 8, step(late or body), 0)


def attend_tile(i, bound, q_ref, g_ref, k_ref, v_ref, kt_ref, vt_ref, o_ref, dq_ref,
                dk_acc, dv_acc, s_buf, o_acc, dq_acc):
    subs = TILE // SUB
    wide = PAIR * SUB
    total = PAIR * TILE
    start = pl.multiple_of(i * TILE, TILE)

    def at(a):
        return pl.ds(pl.multiple_of(start + a * SUB, SUB), SUB)

    def gather(ref):
        return jnp.concatenate([ref[h, at(a), :] for a in range(subs) for h in range(PAIR)], 0)

    q = gather(q_ref)
    g = gather(g_ref)
    row = start + jnp.concatenate(
        [lax.broadcasted_iota(jnp.int32, (8, SUB), 1) + a * SUB
         for a in range(subs) for _ in range(PAIR)], 1)

    def scores(k0, count, first, diagonal, maxima):
        lane0 = first * wide
        maxima = list(maxima)
        for t in range(0, count, 128):
            c0 = pl.multiple_of(k0 + t, 128)
            s = by_eight(dot(k_ref[pl.ds(c0, 128), :], q[lane0:], 1, 1))
            limit = jnp.where(c0 < bound, bound, FAR)
            s = s + jnp.where(row[:, lane0:] >= limit, MASKED, 0.0)[None]
            for a in range(first, subs):
                part = s[:, :, (a - first) * wide:(a - first + 1) * wide]
                if diagonal and a == first:
                    key = (lax.broadcasted_iota(jnp.int32, part.shape, 0) * 8
                           + lax.broadcasted_iota(jnp.int32, part.shape, 1) + c0)
                    part = jnp.where(key > row[None, :, a * wide:(a + 1) * wide], MASKED, part)
                s_buf[pl.ds(c0, 128), a * wide:(a + 1) * wide] = part.reshape(128, wide)
                maxima[a] = jnp.maximum(maxima[a], jnp.max(part, axis=0))
        return tuple(maxima)

    def sweep(body, carry):
        carry = lax.fori_loop(
            0, i, lambda kb, x: body(pl.multiple_of(kb * TILE, TILE), TILE, 0, False, x), carry)
        for a in range(subs):
            carry = body(pl.multiple_of(start + a * SUB, SUB), SUB, a, True, carry)
        return carry

    maxima = sweep(scores, tuple(jnp.full((8, wide), MASKED, F32) for _ in range(subs)))
    top = jnp.concatenate([over_rows(x, jnp.max) * SCALE2 for x in maxima], 1)

    def powers(k0, count, first, diagonal, sums):
        lane0 = first * wide
        p = jnp.exp2(by_eight(s_buf[pl.ds(k0, count), lane0:]) * SCALE2 - top[None, :, lane0:])
        s_buf[pl.ds(k0, count), lane0:] = p.reshape(count, total - lane0)
        added = jnp.sum(p, axis=0)
        return tuple(
            x if a < first else x + added[:, (a - first) * wide:(a - first + 1) * wide]
            for a, x in enumerate(sums))

    sums = sweep(powers, tuple(jnp.zeros((8, wide), F32) for _ in range(subs)))
    inverse = jnp.concatenate([1.0 / over_rows(x, jnp.sum) for x in sums], 1)

    o_acc[...] = jnp.zeros_like(o_acc)

    def outputs(k0, count, first, diagonal, carry):
        lane0 = first * wide
        w = by_eight(s_buf[pl.ds(k0, count), lane0:]) * inverse[None, :, lane0:]
        w = w.reshape(count, total - lane0).astype(BF16)
        o_acc[:, lane0:] += dot(vt_ref[:, pl.ds(k0, count)], w, 1, 0)
        dv_acc[pl.ds(k0, count), :] += dot(w, g[lane0:], 1, 0)
        return carry

    sweep(outputs, 0)
    out = o_acc[...].astype(BF16)

    def put(ref, x):
        x = x.T
        for a in range(subs):
            for h in range(PAIR):
                ref[h, at(a), :] = x[(a * PAIR + h) * SUB:(a * PAIR + h + 1) * SUB]

    put(o_ref, out)
    product = over_rows(g.T.astype(F32) * out.astype(F32), jnp.sum)
    dq_acc[...] = jnp.zeros_like(dq_acc)

    def backward(k0, count, first, diagonal, carry):
        lane0 = first * wide
        dp = by_eight(dot(v_ref[pl.ds(k0, count), :], g[lane0:], 1, 1))
        w = by_eight(s_buf[pl.ds(k0, count), lane0:]) * inverse[None, :, lane0:]
        ds = (w * (dp - product[None, :, lane0:])).reshape(count, total - lane0).astype(BF16)
        dq_acc[:, lane0:] += dot(kt_ref[:, pl.ds(k0, count)], ds, 1, 0)
        dk_acc[pl.ds(k0, count), :] += dot(ds, q[lane0:], 1, 0)
        return carry

    sweep(backward, 0)
    put(dq_ref, (dq_acc[...] * SCALE).astype(BF16))


def attend_short(lengths_ref, q_ref, k_ref, v_ref, g_ref, o_ref, dq_ref, dk_ref, dv_ref):
    heads = HQ // HK
    lanes = heads * SHORT_DEV
    key = lax.broadcasted_iota(jnp.int32, (SHORT_DEV, lanes), 0)
    row = jnp.concatenate(
        [lax.broadcasted_iota(jnp.int32, (SHORT_DEV, SHORT_DEV), 1)] * heads, 1)
    end = 0
    key_segment = jnp.zeros_like(key)
    row_segment = jnp.zeros_like(row)
    for j in range(4):
        end = end + lengths_ref[0, j]
        key_segment = key_segment + (key >= end).astype(jnp.int32)
        row_segment = row_segment + (row >= end).astype(jnp.int32)
    masked = jnp.where((key > row) | (key_segment != row_segment), MASKED, 0.0)

    def one(c, carry):
        mine = pl.ds(pl.multiple_of(c * DH, DH), DH)

        def col(h):
            return pl.ds(pl.multiple_of((c * heads + h) * DH, DH), DH)

        def gather(ref):
            return jnp.concatenate([ref[:SHORT_DEV, col(h)] for h in range(heads)], 0)

        q = gather(q_ref)
        g = gather(g_ref)
        k = k_ref[:SHORT_DEV, mine]
        v = v_ref[:SHORT_DEV, mine]
        s = dot(k, q, 1, 1) + masked
        p = jnp.exp2((s - jnp.max(s, axis=0, keepdims=True)) * SCALE2)
        weights = p * (1.0 / jnp.sum(p, axis=0, keepdims=True))
        w = weights.astype(BF16)
        out = dot(v.T, w, 1, 0).astype(BF16)
        dv_ref[:, mine] = dot(w, g, 1, 0).astype(BF16)
        product = jnp.sum(g.T.astype(F32) * out.astype(F32), axis=0, keepdims=True)
        ds = (weights * (dot(v, g, 1, 1) - product)).astype(BF16)
        dq = (dot(k.T, ds, 1, 0) * SCALE).astype(BF16)
        dk_ref[:, mine] = (dot(ds, q, 1, 0) * SCALE).astype(BF16)
        out = out.T
        dq = dq.T
        for h in range(heads):
            o_ref[:, col(h)] = out[h * SHORT_DEV:(h + 1) * SHORT_DEV]
            dq_ref[:, col(h)] = dq[h * SHORT_DEV:(h + 1) * SHORT_DEV]
        return carry

    lax.fori_loop(0, HK, one, 0)


def kernel(lengths_ref, doc_len_ref, doc_group_ref, doc_off_ref, q_hbm, k_hbm, v_hbm, g_hbm,
           back_a, back_b, so_hbm, sdq_hbm, sdk_hbm, sdv_hbm,
           q_ref, k_ref, v_ref, g_ref, so_ref, sdq_ref, sdk_ref, sdv_ref, send_a, send_b, got_a, got_b, qd, gd, kd, vd, kt, vt, od, dqd,
           dk_acc, dv_acc, s_buf, o_acc, dq_acc, edge,
           send_sem, recv_sem, own_sem, load_sem):
    dp = lax.axis_index("dp")
    ctx = lax.axis_index("ctx")
    me = dp * 4 + ctx
    my_place = position_of(dp, ctx)
    barrier = pltpu.get_barrier_semaphore()

    def greet(*to):
        pl.semaphore_signal(barrier, inc=1, device_id=to, device_id_type=MESH)

    each_partner(dp, ctx, greet)
    loads = [
        pltpu.make_async_copy(src, dst, load_sem.at[n])
        for n, (src, dst) in enumerate(
            ((q_hbm, q_ref), (g_hbm, g_ref), (k_hbm, k_ref), (v_hbm, v_ref)))]
    for load in loads:
        load.start()

    def pack(out, first, with_keys):
        def body(b, carry):
            base = pl.multiple_of(SHORT_DEV + SLAB * b, 16)
            for c in range(HK):
                col = (c * (HQ // HK) + first) * DH
                parts = [(q_ref, col), (q_ref, col + DH), (g_ref, col), (g_ref, col + DH)]
                if with_keys:
                    parts += [(k_ref, c * DH), (v_ref, c * DH)]
                for n, (ref, at) in enumerate(parts):
                    x = ref[pl.ds(base, SLAB), at:at + DH]
                    for j in range(8):
                        out[(b * 8 + j) * 4 + c, PIECE * n:PIECE * (n + 1), :] = (
                            x[PIECE * j:PIECE * (j + 1)])
            return carry

        lax.fori_loop(0, GROUPS // 8, body, 0)

    def exchange(slot, src, dst, src_index, dst_index):
        def send_on(recv):
            def send(*to):
                pltpu.make_async_remote_copy(
                    src_ref=src.at[src_index(*to)], dst_ref=dst.at[dst_index],
                    send_sem=send_sem.at[slot], recv_sem=recv_sem.at[recv],
                    device_id=to, device_id_type=MESH).start()

            return send

        each_partner(dp, ctx, send_on(slot), send_on(slot + 4) if slot < 2 else None)
        pltpu.make_async_copy(
            src.at[src_index(dp, ctx)], dst.at[dst_index], own_sem.at[slot]).start()

    def wait_bytes(ref, sem, count=N_DEV - 1):
        whole = ref.at[pl.ds(0, count)]
        pltpu.make_async_copy(whole, whole, sem).wait()

    def own_copy(slot, src, dst):
        return pltpu.make_async_copy(src.at[0], dst.at[0], own_sem.at[slot])

    def mostly_received(slot, dst):
        wait_bytes(dst, recv_sem.at[slot], 16 * EARLY - 1)

    def received(slot, src, dst):
        own_copy(slot, src, dst).wait()
        if slot < 2:
            wait_bytes(dst, recv_sem.at[slot + 4], 16 * (8 - EARLY))
        else:
            wait_bytes(dst, recv_sem.at[slot])

    send_a[:, 96:, :] = jnp.zeros((N_DEV, ROWS_A - 96, DH), BF16)
    for load in loads:
        load.wait()
    pack(send_a, 0, True)
    pl.semaphore_wait(barrier, N_DEV - 1)
    exchange(0, send_a, got_a, lambda d, c: d * 4 + c, my_place)
    pack(send_b, PAIR, False)
    attend_short(lengths_ref, q_ref, k_ref, v_ref, g_ref, so_ref, sdq_ref, sdk_ref, sdv_ref)
    stores = [
        pltpu.make_async_copy(src, dst, load_sem.at[4 + n])
        for n, (src, dst) in enumerate(
            ((so_ref, so_hbm), (sdq_ref, sdq_hbm), (sdk_ref, sdk_hbm), (sdv_ref, sdv_hbm)))]
    for store in stores:
        store.start()

    def find(i, acc):
        mine = (doc_group_ref[i] == dp) & (doc_len_ref[i] > 0)
        return acc + jnp.where(mine, doc_off_ref[i], 0)

    bound = lax.fori_loop(0, doc_len_ref.shape[0], find, jnp.int32(0))
    dk_acc[...] = jnp.zeros_like(dk_acc)
    dv_acc[...] = jnp.zeros_like(dv_acc)

    def spread(src, dests):
        def body(b, carry):
            at = pl.ds(pl.multiple_of(b * SLAB, 16), SLAB)
            for n, (ref, h) in enumerate(dests):
                for j in range(8):
                    edge[n, PIECE * j:PIECE * (j + 1), :] = (
                        src[b * 8 + j, PIECE * n:PIECE * (n + 1), :])
                if h is None:
                    ref[at, :] = edge[n]
                else:
                    ref[h, at, :] = edge[n]
            return carry

        lax.fori_loop(0, N_DEV // 8, body, 0)

    def collect(out, load):
        def body(b, carry):
            at = pl.ds(pl.multiple_of(b * SLAB, 16), SLAB)
            for n, x in enumerate(load(at)):
                for j in range(8):
                    out[b * 8 + j, PIECE * n:PIECE * (n + 1), :] = x[PIECE * j:PIECE * (j + 1)]
            return carry

        lax.fori_loop(0, N_DEV // 8, body, 0)

    def attend():
        def body(i, carry):
            attend_tile(i, bound, qd, gd, kd, vd, kt, vt, od, dqd,
                        dk_acc, dv_acc, s_buf, o_acc, dq_acc)
            return carry

        lax.fori_loop(0, SPAN // TILE, body, 0)

    query_side = [(qd, 0), (qd, 1), (gd, 0), (gd, 1)]
    mostly_received(0, got_a)
    exchange(1, send_b, got_b, lambda d, c: d * 4 + c, my_place)
    received(0, send_a, got_a)
    spread(got_a, query_side + [(kd, None), (vd, None)])
    kt[...] = kd[...].T
    vt[...] = vd[...].T
    attend()

    wait_bytes(send_b, send_sem.at[1])
    own_copy(1, send_b, got_b).wait()
    collect(send_b, lambda at: [od[0, at, :], od[1, at, :], dqd[0, at, :], dqd[1, at, :]])
    mostly_received(1, got_b)
    exchange(2, send_b, back_a, position_of, me)
    wait_bytes(got_b, recv_sem.at[5], 16 * (8 - EARLY))
    spread(got_b, query_side)
    attend()
    wait_bytes(send_a, send_sem.at[0])
    collect(send_a, lambda at: [
        od[0, at, :], od[1, at, :], dqd[0, at, :], dqd[1, at, :],
        (dk_acc[at, :] * SCALE).astype(BF16), dv_acc[at, :].astype(BF16)])
    exchange(3, send_a, back_b, position_of, me)

    for store in stores:
        store.wait()
    received(2, send_b, back_a)
    wait_bytes(send_b, send_sem.at[2])
    received(3, send_a, back_b)
    wait_bytes(send_a, send_sem.at[3])


def place(back_a, back_b, so_ref, sdq_ref, sdk_ref, sdv_ref, o_ref, dq_ref, dk_ref, dv_ref):
    o_ref[:SHORT_DEV, :] = so_ref[...]
    dq_ref[:SHORT_DEV, :] = sdq_ref[...]
    dk_ref[:SHORT_DEV, :] = sdk_ref[...]
    dv_ref[:SHORT_DEV, :] = sdv_ref[...]
    moves = []
    for half, src in enumerate((back_a, back_b)):
        for n, ref in enumerate((o_ref, o_ref, dq_ref, dq_ref)):
            moves.append((src, n, ref, (half * 2 + n % 2) * DH))
    moves += [(back_b, 4, dk_ref, 0), (back_b, 5, dv_ref, 0)]

    for g in range(GROUPS):
        at = SHORT_DEV + PIECE * g
        for src, n, ref, col in moves:
            ref[at:at + PIECE, col:col + DH] = src[g, 0, PIECE * n:PIECE * (n + 1), :]


def per_device(queries, keys, values, out_grad, short_lengths, doc_lengths, doc_group, doc_offset):
    smem = pl.BlockSpec(memory_space=pltpu.SMEM)
    hbm = pl.BlockSpec(memory_space=pl.ANY)

    def shape(*dims):
        return jax.ShapeDtypeStruct(dims, BF16)

    results = pl.pallas_call(
        kernel,
        out_shape=[
            shape(N_DEV, ROWS_B, DH), shape(N_DEV, ROWS_A, DH),
            shape(SHORT_DEV, HQ * DH), shape(SHORT_DEV, HQ * DH),
            shape(SHORT_DEV, HK * DH), shape(SHORT_DEV, HK * DH)],
        in_specs=[smem] * 4 + [hbm] * 4,
        out_specs=[hbm] * 6,
        scratch_shapes=[
            pltpu.VMEM((ROWS, HQ * DH), BF16), pltpu.VMEM((ROWS, HK * DH), BF16),
            pltpu.VMEM((ROWS, HK * DH), BF16), pltpu.VMEM((ROWS, HQ * DH), BF16),
            pltpu.VMEM((SHORT_DEV, HQ * DH), BF16), pltpu.VMEM((SHORT_DEV, HQ * DH), BF16),
            pltpu.VMEM((SHORT_DEV, HK * DH), BF16), pltpu.VMEM((SHORT_DEV, HK * DH), BF16),
            pltpu.VMEM((N_DEV, ROWS_A, DH), BF16), pltpu.VMEM((N_DEV, ROWS_B, DH), BF16),
            pltpu.VMEM((N_DEV, ROWS_A, DH), BF16), pltpu.VMEM((N_DEV, ROWS_B, DH), BF16),
            pltpu.VMEM((PAIR, SPAN, DH), BF16), pltpu.VMEM((PAIR, SPAN, DH), BF16),
            pltpu.VMEM((SPAN, DH), BF16), pltpu.VMEM((SPAN, DH), BF16),
            pltpu.VMEM((DH, SPAN), BF16), pltpu.VMEM((DH, SPAN), BF16),
            pltpu.VMEM((PAIR, SPAN, DH), BF16), pltpu.VMEM((PAIR, SPAN, DH), BF16),
            pltpu.VMEM((SPAN, DH), F32), pltpu.VMEM((SPAN, DH), F32),
            pltpu.VMEM((SPAN, PAIR * TILE), F32),
            pltpu.VMEM((DH, PAIR * TILE), F32), pltpu.VMEM((DH, PAIR * TILE), F32),
            pltpu.VMEM((6, SLAB, DH), BF16),
            pltpu.SemaphoreType.DMA((4,)), pltpu.SemaphoreType.DMA((6,)),
            pltpu.SemaphoreType.DMA((4,)), pltpu.SemaphoreType.DMA((8,))],
        compiler_params=pltpu.CompilerParams(
            collective_id=0, has_side_effects=True, vmem_limit_bytes=60 << 20),
        name="relay_and_attend",
    )(short_lengths, doc_lengths, doc_group, doc_offset, queries, keys, values, out_grad)

    back_a, back_b, *short = results
    heads = HQ // HK

    def back_spec(rows):
        return pl.BlockSpec((GROUPS, 1, rows, DH), lambda c: (0, c, 0, 0))

    def col_spec(rows, width):
        return pl.BlockSpec((rows, width), lambda c: (0, c))

    return tuple(pl.pallas_call(
        place,
        grid=(HK,),
        out_shape=[shape(ROWS, HQ * DH), shape(ROWS, HQ * DH),
                   shape(ROWS, HK * DH), shape(ROWS, HK * DH)],
        in_specs=[back_spec(ROWS_B), back_spec(ROWS_A),
                  col_spec(SHORT_DEV, heads * DH), col_spec(SHORT_DEV, heads * DH),
                  col_spec(SHORT_DEV, DH), col_spec(SHORT_DEV, DH)],
        out_specs=[col_spec(ROWS, heads * DH), col_spec(ROWS, heads * DH),
                   col_spec(ROWS, DH), col_spec(ROWS, DH)],
        compiler_params=pltpu.CompilerParams(vmem_limit_bytes=60 << 20),
        name="place_outputs",
    )(back_a.reshape(GROUPS, N_DEV // GROUPS, ROWS_B, DH),
      back_b.reshape(GROUPS, N_DEV // GROUPS, ROWS_A, DH), *short))


def solution(mesh):
    rows = P(("dp", "ctx"), None)
    return jax.shard_map(
        per_device, mesh=mesh,
        in_specs=(rows, rows, rows, rows, rows, P(), P(), P()),
        out_specs=(rows, rows, rows, rows), check_vma=False)
```

```python
import functools
import math

import jax
import jax.numpy as jnp
from jax import lax
from jax.experimental import pallas as pl
from jax.experimental.pallas import tpu as pltpu
from jax.sharding import PartitionSpec as P

HQ = 16
HK = 4
DH = 128
SHORT_DEV = 128
LONG_DEV = 576
ROWS = SHORT_DEV + LONG_DEV

N_DEV = 128
GROUPS = 32
PIECE = LONG_DEV // GROUPS
SLAB = 8 * PIECE
SPAN = N_DEV * PIECE
PAIR = 2
TILE = 768
SUB = 256
ROWS_A = 112
ROWS_B = 72

SCALE = 1.0 / math.sqrt(DH)
SCALE2 = math.log2(math.e) / math.sqrt(DH)
MASKED = -1e30
FAR = 1 << 20
F32 = jnp.float32
BF16 = jnp.bfloat16
MESH = pl.DeviceIdType.MESH


def dot(a, b, dim_a, dim_b):
    return lax.dot_general(
        a, b, (((dim_a,), (dim_b,)), ((), ())), preferred_element_type=F32
    )


def by_eight(x):
    return x.reshape(x.shape[0] // 8, 8, x.shape[1])


def over_rows(x, op):
    return jnp.broadcast_to(op(x, axis=0, keepdims=True), (8, x.shape[1]))


def position_of(dp, ctx):
    return jnp.where(dp < 16, ctx * 16 + dp, (7 - ctx) * 16 + dp - 16)


EARLY = 7

TURNS = ((1, 0), (0, 1), (3, 0), (0, 3), (1, 3), (3, 1), (2, 2), (0, 2),
         (2, 0), (1, 1), (3, 3), (1, 2), (3, 2), (2, 1), (2, 3), (0, 0))


def each_partner(dp, ctx, body, late=None):
    def wrap(value, size):
        return jnp.where(value >= size, value - size, value)

    xs = [wrap(ctx + i, 4) for i in range(4)]
    ys = [wrap(lax.rem(dp // 2, 4) + i, 4) * 2 for i in range(4)]

    def turn(j, turns, body):
        z = wrap(dp // 8 + lax.rem(j, 4), 4)
        core = wrap(lax.rem(dp, 2) + j // 4, 2)
        zs = [wrap(z + i, 4) * 8 for i in range(4)]
        cores = [core, 1 - core]
        for x, y in turns:
            body(zs[(x + y) % 4] + ys[y] + cores[x % 2], xs[x])

    def step(call):
        def one(j, carry):
            turn(j, TURNS, call)
            return carry

        return one

    turn(0, TURNS[:-1], body)
    lax.fori_loop(1, EARLY, step(body), 0)
    lax.fori_loop(EARLY, 8, step(late or body), 0)


def attend_tile(i, bound, q_ref, g_ref, k_ref, v_ref, kt_ref, vt_ref, o_ref, dq_ref,
                dk_acc, dv_acc, s_buf, o_acc, dq_acc):
    subs = TILE // SUB
    wide = PAIR * SUB
    total = PAIR * TILE
    start = pl.multiple_of(i * TILE, TILE)

    def at(a):
        return pl.ds(pl.multiple_of(start + a * SUB, SUB), SUB)

    def gather(ref):
        return jnp.concatenate([ref[h, at(a), :] for a in range(subs) for h in range(PAIR)], 0)

    q = gather(q_ref)
    g = gather(g_ref)
    row = start + jnp.concatenate(
        [lax.broadcasted_iota(jnp.int32, (8, SUB), 1) + a * SUB
         for a in range(subs) for _ in range(PAIR)], 1)

    def scores(k0, count, first, diagonal, maxima):
        lane0 = first * wide
        maxima = list(maxima)
        for t in range(0, count, 128):
            c0 = pl.multiple_of(k0 + t, 128)
            s = by_eight(dot(k_ref[pl.ds(c0, 128), :], q[lane0:], 1, 1))
            limit = jnp.where(c0 < bound, bound, FAR)
            s = s + jnp.where(row[:, lane0:] >= limit, MASKED, 0.0)[None]
            for a in range(first, subs):
                part = s[:, :, (a - first) * wide:(a - first + 1) * wide]
                if diagonal and a == first:
                    key = (lax.broadcasted_iota(jnp.int32, part.shape, 0) * 8
                           + lax.broadcasted_iota(jnp.int32, part.shape, 1) + c0)
                    part = jnp.where(key > row[None, :, a * wide:(a + 1) * wide], MASKED, part)
                s_buf[pl.ds(c0, 128), a * wide:(a + 1) * wide] = part.reshape(128, wide)
                maxima[a] = jnp.maximum(maxima[a], jnp.max(part, axis=0))
        return tuple(maxima)

    def sweep(body, carry):
        carry = lax.fori_loop(
            0, i, lambda kb, x: body(pl.multiple_of(kb * TILE, TILE), TILE, 0, False, x), carry)
        for a in range(subs):
            carry = body(pl.multiple_of(start + a * SUB, SUB), SUB, a, True, carry)
        return carry

    maxima = sweep(scores, tuple(jnp.full((8, wide), MASKED, F32) for _ in range(subs)))
    top = jnp.concatenate([over_rows(x, jnp.max) * SCALE2 for x in maxima], 1)

    def powers(k0, count, first, diagonal, sums):
        lane0 = first * wide
        p = jnp.exp2(by_eight(s_buf[pl.ds(k0, count), lane0:]) * SCALE2 - top[None, :, lane0:])
        s_buf[pl.ds(k0, count), lane0:] = p.reshape(count, total - lane0)
        added = jnp.sum(p, axis=0)
        return tuple(
            x if a < first else x + added[:, (a - first) * wide:(a - first + 1) * wide]
            for a, x in enumerate(sums))

    sums = sweep(powers, tuple(jnp.zeros((8, wide), F32) for _ in range(subs)))
    inverse = jnp.concatenate([1.0 / over_rows(x, jnp.sum) for x in sums], 1)

    o_acc[...] = jnp.zeros_like(o_acc)

    def outputs(k0, count, first, diagonal, carry):
        lane0 = first * wide
        w = by_eight(s_buf[pl.ds(k0, count), lane0:]) * inverse[None, :, lane0:]
        w = w.reshape(count, total - lane0).astype(BF16)
        o_acc[:, lane0:] += dot(vt_ref[:, pl.ds(k0, count)], w, 1, 0)
        dv_acc[pl.ds(k0, count), :] += dot(w, g[lane0:], 1, 0)
        return carry

    sweep(outputs, 0)
    out = o_acc[...].astype(BF16)

    def put(ref, x):
        x = x.T
        for a in range(subs):
            for h in range(PAIR):
                ref[h, at(a), :] = x[(a * PAIR + h) * SUB:(a * PAIR + h + 1) * SUB]

    put(o_ref, out)
    product = over_rows(g.T.astype(F32) * out.astype(F32), jnp.sum)
    dq_acc[...] = jnp.zeros_like(dq_acc)

    def backward(k0, count, first, diagonal, carry):
        lane0 = first * wide
        dp = by_eight(dot(v_ref[pl.ds(k0, count), :], g[lane0:], 1, 1))
        w = by_eight(s_buf[pl.ds(k0, count), lane0:]) * inverse[None, :, lane0:]
        ds = (w * (dp - product[None, :, lane0:])).reshape(count, total - lane0).astype(BF16)
        dq_acc[:, lane0:] += dot(kt_ref[:, pl.ds(k0, count)], ds, 1, 0)
        dk_acc[pl.ds(k0, count), :] += dot(ds, q[lane0:], 1, 0)
        return carry

    sweep(backward, 0)
    put(dq_ref, (dq_acc[...] * SCALE).astype(BF16))


def attend_short(lengths_ref, q_ref, k_ref, v_ref, g_ref, o_ref, dq_ref, dk_ref, dv_ref):
    heads = HQ // HK
    lanes = heads * SHORT_DEV
    key = lax.broadcasted_iota(jnp.int32, (SHORT_DEV, lanes), 0)
    row = jnp.concatenate(
        [lax.broadcasted_iota(jnp.int32, (SHORT_DEV, SHORT_DEV), 1)] * heads, 1)
    end = 0
    key_segment = jnp.zeros_like(key)
    row_segment = jnp.zeros_like(row)
    for j in range(4):
        end = end + lengths_ref[0, j]
        key_segment = key_segment + (key >= end).astype(jnp.int32)
        row_segment = row_segment + (row >= end).astype(jnp.int32)
    masked = jnp.where((key > row) | (key_segment != row_segment), MASKED, 0.0)

    def one(c, carry):
        mine = pl.ds(pl.multiple_of(c * DH, DH), DH)

        def col(h):
            return pl.ds(pl.multiple_of((c * heads + h) * DH, DH), DH)

        def gather(ref):
            return jnp.concatenate([ref[:SHORT_DEV, col(h)] for h in range(heads)], 0)

        q = gather(q_ref)
        g = gather(g_ref)
        k = k_ref[:SHORT_DEV, mine]
        v = v_ref[:SHORT_DEV, mine]
        s = dot(k, q, 1, 1) + masked
        p = jnp.exp2((s - jnp.max(s, axis=0, keepdims=True)) * SCALE2)
        weights = p * (1.0 / jnp.sum(p, axis=0, keepdims=True))
        w = weights.astype(BF16)
        out = dot(v.T, w, 1, 0).astype(BF16)
        dv_ref[:, mine] = dot(w, g, 1, 0).astype(BF16)
        product = jnp.sum(g.T.astype(F32) * out.astype(F32), axis=0, keepdims=True)
        ds = (weights * (dot(v, g, 1, 1) - product)).astype(BF16)
        dq = (dot(k.T, ds, 1, 0) * SCALE).astype(BF16)
        dk_ref[:, mine] = (dot(ds, q, 1, 0) * SCALE).astype(BF16)
        out = out.T
        dq = dq.T
        for h in range(heads):
            o_ref[:, col(h)] = out[h * SHORT_DEV:(h + 1) * SHORT_DEV]
            dq_ref[:, col(h)] = dq[h * SHORT_DEV:(h + 1) * SHORT_DEV]
        return carry

    lax.fori_loop(0, HK, one, 0)


def kernel(lengths_ref, doc_len_ref, doc_group_ref, doc_off_ref, q_hbm, k_hbm, v_hbm, g_hbm,
           back_a, back_b, so_hbm, sdq_hbm, sdk_hbm, sdv_hbm,
           q_ref, k_ref, v_ref, g_ref, so_ref, sdq_ref, sdk_ref, sdv_ref, send_a, send_b, got_a, got_b, qd, gd, kd, vd, kt, vt, od, dqd,
           dk_acc, dv_acc, s_buf, o_acc, dq_acc, edge,
           send_sem, recv_sem, own_sem, load_sem):
    dp = lax.axis_index("dp")
    ctx = lax.axis_index("ctx")
    me = dp * 4 + ctx
    my_place = position_of(dp, ctx)
    barrier = pltpu.get_barrier_semaphore()

    def greet(*to):
        pl.semaphore_signal(barrier, inc=1, device_id=to, device_id_type=MESH)

    each_partner(dp, ctx, greet)
    loads = [
        pltpu.make_async_copy(src, dst, load_sem.at[n])
        for n, (src, dst) in enumerate(
            ((q_hbm, q_ref), (g_hbm, g_ref), (k_hbm, k_ref), (v_hbm, v_ref)))]
    for load in loads:
        load.start()

    def pack(out, first, with_keys):
        def body(b, carry):
            base = pl.multiple_of(SHORT_DEV + SLAB * b, 16)
            for c in range(HK):
                col = (c * (HQ // HK) + first) * DH
                parts = [(q_ref, col), (q_ref, col + DH), (g_ref, col), (g_ref, col + DH)]
                if with_keys:
                    parts += [(k_ref, c * DH), (v_ref, c * DH)]
                for n, (ref, at) in enumerate(parts):
                    x = ref[pl.ds(base, SLAB), at:at + DH]
                    for j in range(8):
                        out[(b * 8 + j) * 4 + c, PIECE * n:PIECE * (n + 1), :] = (
                            x[PIECE * j:PIECE * (j + 1)])
            return carry

        lax.fori_loop(0, GROUPS // 8, body, 0)

    def exchange(slot, src, dst, src_index, dst_index):
        def send_on(recv):
            def send(*to):
                pltpu.make_async_remote_copy(
                    src_ref=src.at[src_index(*to)], dst_ref=dst.at[dst_index],
                    send_sem=send_sem.at[slot], recv_sem=recv_sem.at[recv],
                    device_id=to, device_id_type=MESH).start()

            return send

        each_partner(dp, ctx, send_on(slot), send_on(slot + 4) if slot < 2 else None)
        pltpu.make_async_copy(
            src.at[src_index(dp, ctx)], dst.at[dst_index], own_sem.at[slot]).start()

    def wait_bytes(ref, sem, count=N_DEV - 1):
        whole = ref.at[pl.ds(0, count)]
        pltpu.make_async_copy(whole, whole, sem).wait()

    def own_copy(slot, src, dst):
        return pltpu.make_async_copy(src.at[0], dst.at[0], own_sem.at[slot])

    def mostly_received(slot, dst):
        wait_bytes(dst, recv_sem.at[slot], 16 * EARLY - 1)

    def received(slot, src, dst):
        own_copy(slot, src, dst).wait()
        if slot < 2:
            wait_bytes(dst, recv_sem.at[slot + 4], 16 * (8 - EARLY))
        else:
            wait_bytes(dst, recv_sem.at[slot])

    send_a[:, 96:, :] = jnp.zeros((N_DEV, ROWS_A - 96, DH), BF16)
    for load in loads:
        load.wait()
    pack(send_a, 0, True)
    pl.semaphore_wait(barrier, N_DEV - 1)
    exchange(0, send_a, got_a, lambda d, c: d * 4 + c, my_place)
    pack(send_b, PAIR, False)
    attend_short(lengths_ref, q_ref, k_ref, v_ref, g_ref, so_ref, sdq_ref, sdk_ref, sdv_ref)
    stores = [
        pltpu.make_async_copy(src, dst, load_sem.at[4 + n])
        for n, (src, dst) in enumerate(
            ((so_ref, so_hbm), (sdq_ref, sdq_hbm), (sdk_ref, sdk_hbm), (sdv_ref, sdv_hbm)))]
    for store in stores:
        store.start()

    def find(i, acc):
        mine = (doc_group_ref[i] == dp) & (doc_len_ref[i] > 0)
        return acc + jnp.where(mine, doc_off_ref[i], 0)

    bound = lax.fori_loop(0, doc_len_ref.shape[0], find, jnp.int32(0))
    dk_acc[...] = jnp.zeros_like(dk_acc)
    dv_acc[...] = jnp.zeros_like(dv_acc)

    def spread(src, dests):
        def body(b, carry):
            at = pl.ds(pl.multiple_of(b * SLAB, 16), SLAB)
            for n, (ref, h) in enumerate(dests):
                for j in range(8):
                    edge[n, PIECE * j:PIECE * (j + 1), :] = (
                        src[b * 8 + j, PIECE * n:PIECE * (n + 1), :])
                if h is None:
                    ref[at, :] = edge[n]
                else:
                    ref[h, at, :] = edge[n]
            return carry

        lax.fori_loop(0, N_DEV // 8, body, 0)

    def collect(out, load):
        def body(b, carry):
            at = pl.ds(pl.multiple_of(b * SLAB, 16), SLAB)
            for n, x in enumerate(load(at)):
                for j in range(8):
                    out[b * 8 + j, PIECE * n:PIECE * (n + 1), :] = x[PIECE * j:PIECE * (j + 1)]
            return carry

        lax.fori_loop(0, N_DEV // 8, body, 0)

    def attend():
        def body(i, carry):
            attend_tile(i, bound, qd, gd, kd, vd, kt, vt, od, dqd,
                        dk_acc, dv_acc, s_buf, o_acc, dq_acc)
            return carry

        lax.fori_loop(0, SPAN // TILE, body, 0)

    query_side = [(qd, 0), (qd, 1), (gd, 0), (gd, 1)]
    mostly_received(0, got_a)
    exchange(1, send_b, got_b, lambda d, c: d * 4 + c, my_place)
    received(0, send_a, got_a)
    spread(got_a, query_side + [(kd, None), (vd, None)])
    kt[...] = kd[...].T
    vt[...] = vd[...].T
    attend()

    wait_bytes(send_b, send_sem.at[1])
    own_copy(1, send_b, got_b).wait()
    collect(send_b, lambda at: [od[0, at, :], od[1, at, :], dqd[0, at, :], dqd[1, at, :]])
    mostly_received(1, got_b)
    exchange(2, send_b, back_a, position_of, me)
    wait_bytes(got_b, recv_sem.at[5], 16 * (8 - EARLY))
    spread(got_b, query_side)
    attend()
    wait_bytes(send_a, send_sem.at[0])
    collect(send_a, lambda at: [
        od[0, at, :], od[1, at, :], dqd[0, at, :], dqd[1, at, :],
        (dk_acc[at, :] * SCALE).astype(BF16), dv_acc[at, :].astype(BF16)])
    exchange(3, send_a, back_b, position_of, me)

    for store in stores:
        store.wait()
    received(2, send_b, back_a)
    wait_bytes(send_b, send_sem.at[2])
    received(3, send_a, back_b)
    wait_bytes(send_a, send_sem.at[3])


def place(back_a, back_b, so_ref, sdq_ref, sdk_ref, sdv_ref, o_ref, dq_ref, dk_ref, dv_ref,
          a_buf, b_buf, o_buf, dq_buf, dk_buf, dv_buf, so_buf, sdq_buf, sdk_buf, sdv_buf,
          in_sem, out_sem, short_sem):
    heads = HQ // HK
    steps = GROUPS // 8
    slots = N_DEV // steps
    shorts = ((so_ref, so_buf, o_ref), (sdq_ref, sdq_buf, dq_ref),
              (sdk_ref, sdk_buf, dk_ref), (sdv_ref, sdv_buf, dv_ref))
    fetched = [
        pltpu.make_async_copy(src, buf, short_sem.at[0, n])
        for n, (src, buf, _) in enumerate(shorts)]
    loads = []
    for b in range(steps):
        part = pl.ds(b * slots, slots)
        loads.append([
            pltpu.make_async_copy(back_a.at[part], a_buf.at[part], in_sem.at[b, 0]),
            pltpu.make_async_copy(back_b.at[part], b_buf.at[part], in_sem.at[b, 1])])
        for load in loads[b] + (fetched if b == 0 else []):
            load.start()
    moves = []
    for half, src in enumerate((a_buf, b_buf)):
        for n, buf in enumerate((o_buf, o_buf, dq_buf, dq_buf)):
            moves.append((src, n, buf, heads, half * 2 + n % 2))
    moves += [(b_buf, 4, dk_buf, 1, 0), (b_buf, 5, dv_buf, 1, 0)]

    copies = []
    for b in range(steps):
        for load in loads[b]:
            load.wait()

        def columns(c, carry):
            for j in range(8):
                for src, n, buf, width, at in moves:
                    col = pl.multiple_of((c * width + at) * DH, DH)
                    buf[b, PIECE * j:PIECE * (j + 1), pl.ds(col, DH)] = (
                        src[(b * 8 + j) * HK + c, PIECE * n:PIECE * (n + 1), :])
            return carry

        lax.fori_loop(0, HK, columns, 0)
        rows = pl.ds(SHORT_DEV + b * SLAB, SLAB)
        for n, (buf, dst) in enumerate(
                ((o_buf, o_ref), (dq_buf, dq_ref), (dk_buf, dk_ref), (dv_buf, dv_ref))):
            copy = pltpu.make_async_copy(buf.at[b], dst.at[rows], out_sem.at[b, n])
            copy.start()
            copies.append(copy)
        if b == 0:
            for n, (_, buf, dst) in enumerate(shorts):
                fetched[n].wait()
                copy = pltpu.make_async_copy(buf, dst.at[pl.ds(0, SHORT_DEV)], short_sem.at[1, n])
                copy.start()
                copies.append(copy)
    for copy in copies:
        copy.wait()


def per_device(queries, keys, values, out_grad, short_lengths, doc_lengths, doc_group, doc_offset):
    smem = pl.BlockSpec(memory_space=pltpu.SMEM)
    hbm = pl.BlockSpec(memory_space=pl.ANY)

    def shape(*dims):
        return jax.ShapeDtypeStruct(dims, BF16)

    results = pl.pallas_call(
        kernel,
        out_shape=[
            shape(N_DEV, ROWS_B, DH), shape(N_DEV, ROWS_A, DH),
            shape(SHORT_DEV, HQ * DH), shape(SHORT_DEV, HQ * DH),
            shape(SHORT_DEV, HK * DH), shape(SHORT_DEV, HK * DH)],
        in_specs=[smem] * 4 + [hbm] * 4,
        out_specs=[hbm] * 6,
        scratch_shapes=[
            pltpu.VMEM((ROWS, HQ * DH), BF16), pltpu.VMEM((ROWS, HK * DH), BF16),
            pltpu.VMEM((ROWS, HK * DH), BF16), pltpu.VMEM((ROWS, HQ * DH), BF16),
            pltpu.VMEM((SHORT_DEV, HQ * DH), BF16), pltpu.VMEM((SHORT_DEV, HQ * DH), BF16),
            pltpu.VMEM((SHORT_DEV, HK * DH), BF16), pltpu.VMEM((SHORT_DEV, HK * DH), BF16),
            pltpu.VMEM((N_DEV, ROWS_A, DH), BF16), pltpu.VMEM((N_DEV, ROWS_B, DH), BF16),
            pltpu.VMEM((N_DEV, ROWS_A, DH), BF16), pltpu.VMEM((N_DEV, ROWS_B, DH), BF16),
            pltpu.VMEM((PAIR, SPAN, DH), BF16), pltpu.VMEM((PAIR, SPAN, DH), BF16),
            pltpu.VMEM((SPAN, DH), BF16), pltpu.VMEM((SPAN, DH), BF16),
            pltpu.VMEM((DH, SPAN), BF16), pltpu.VMEM((DH, SPAN), BF16),
            pltpu.VMEM((PAIR, SPAN, DH), BF16), pltpu.VMEM((PAIR, SPAN, DH), BF16),
            pltpu.VMEM((SPAN, DH), F32), pltpu.VMEM((SPAN, DH), F32),
            pltpu.VMEM((SPAN, PAIR * TILE), F32),
            pltpu.VMEM((DH, PAIR * TILE), F32), pltpu.VMEM((DH, PAIR * TILE), F32),
            pltpu.VMEM((6, SLAB, DH), BF16),
            pltpu.SemaphoreType.DMA((4,)), pltpu.SemaphoreType.DMA((6,)),
            pltpu.SemaphoreType.DMA((4,)), pltpu.SemaphoreType.DMA((8,))],
        compiler_params=pltpu.CompilerParams(
            collective_id=0, has_side_effects=True, vmem_limit_bytes=60 << 20),
        name="relay_and_attend",
    )(short_lengths, doc_lengths, doc_group, doc_offset, queries, keys, values, out_grad)

    steps = GROUPS // 8
    return tuple(pl.pallas_call(
        place,
        out_shape=[shape(ROWS, HQ * DH), shape(ROWS, HQ * DH),
                   shape(ROWS, HK * DH), shape(ROWS, HK * DH)],
        in_specs=[hbm] * 6,
        out_specs=[hbm] * 4,
        scratch_shapes=[
            pltpu.VMEM((N_DEV, ROWS_B, DH), BF16), pltpu.VMEM((N_DEV, ROWS_A, DH), BF16),
            pltpu.VMEM((steps, SLAB, HQ * DH), BF16), pltpu.VMEM((steps, SLAB, HQ * DH), BF16),
            pltpu.VMEM((steps, SLAB, HK * DH), BF16), pltpu.VMEM((steps, SLAB, HK * DH), BF16),
            pltpu.VMEM((SHORT_DEV, HQ * DH), BF16), pltpu.VMEM((SHORT_DEV, HQ * DH), BF16),
            pltpu.VMEM((SHORT_DEV, HK * DH), BF16), pltpu.VMEM((SHORT_DEV, HK * DH), BF16),
            pltpu.SemaphoreType.DMA((steps, 2)), pltpu.SemaphoreType.DMA((steps, 4)),
            pltpu.SemaphoreType.DMA((2, 4))],
        compiler_params=pltpu.CompilerParams(vmem_limit_bytes=60 << 20),
        name="place_outputs",
    )(*results))


def solution(mesh):
    rows = P(("dp", "ctx"), None)
    return jax.shard_map(
        per_device, mesh=mesh,
        in_specs=(rows, rows, rows, rows, rows, P(), P(), P()),
        out_specs=(rows, rows, rows, rows), check_vma=False)
```
